32 devices in a mesh: dp: 4 (over y, x), row: 2 (over core), col: 4 (over z).
Axes of the slice: x: 2, y: 2, z: 4, core: 2. Of those that a mesh axis runs over, the one named last changes fastest.
Arguments:
- images: bfloat16 [12608, 384], P(('dp', 'row'), 'col'), may hold values from -9 to 9
- cotangent: bfloat16 [12608, 384], P(('dp', 'row'), 'col'), may hold values from -6 to 6
- attn_in: float32 [2, 2, 4, 55296], P(None, 'row', 'col'), may hold values from -0.3125 to 0.3125
- attn_out: float32 [2, 2, 4, 18432], P(None, 'row', 'col'), may hold values from -1.5 to 1.5
- mlp_in: float32 [2, 384, 1536], P(None, 'col', 'row'), may hold values from -0.3125 to 0.3125
- mlp_out: float32 [2, 384, 1536], P(None, 'col', 'row'), may hold values from -0.15625 to 0.15625
- attn_bias: float32 [2, 2, 384], P(None, None, 'row'), may hold values from -1.8 to 1.8
- mlp_bias: float32 [2, 1536], P(None, 'row'), may hold values from -1.8 to 1.8
- norm_vectors: float32 [2, 6, 384], P(None, None, 'col'), may hold values from -0.9 to 1.5
- attn_in_first: float32 [2, 2, 4, 55296], P(None, 'row', 'col'), may hold values from -74.10833 to 74.10833
- attn_out_first: float32 [2, 2, 4, 18432], P(None, 'row', 'col'), may hold values from -9.145228 to 9.145228
- mlp_in_first: float32 [2, 384, 1536], P(None, 'col', 'row'), may hold values from -22.45707 to 22.45707
- mlp_out_first: float32 [2, 384, 1536], P(None, 'col', 'row'), may hold values from -44.91414 to 44.91414
- attn_bias_first: float32 [2, 2, 384], P(None, None, 'row'), may hold values from -74.10833 to 74.10833
- mlp_bias_first: float32 [2, 1536], P(None, 'row'), may hold values from -22.45707 to 22.45707
- norm_vectors_first: float32 [2, 6, 384], P(None, None, 'col'), may hold values from -74.10833 to 74.10833
- attn_in_second: float32 [2, 2, 4, 55296], P(None, 'row', 'col'), may hold values from 6.304 to 100.864
- attn_out_second: float32 [2, 2, 4, 18432], P(None, 'row', 'col'), may hold values from 0.096 to 1.536
- mlp_in_second: float32 [2, 384, 1536], P(None, 'col', 'row'), may hold values from 0.56736 to 9.07776
- mlp_out_second: float32 [2, 384, 1536], P(None, 'col', 'row'), may hold values from 2.26944 to 36.5632
- attn_bias_second: float32 [2, 2, 384], P(None, None, 'row'), may hold values from 6.304 to 100.864
- mlp_bias_second: float32 [2, 1536], P(None, 'row'), may hold values from 0.56736 to 9.07776
- norm_vectors_second: float32 [2, 6, 384], P(None, None, 'col'), may hold values from 6.304 to 100.864
Outputs:
- activations: bfloat16 [12608, 384], P(('dp', 'row'), 'col')
- input_grad: float32 [12608, 384], P(('dp', 'row'), 'col')
- attn_in_new: float32 [2, 2, 4, 55296], P(None, 'row', 'col')
- attn_out_new: float32 [2, 2, 4, 18432], P(None, 'row', 'col')
- mlp_in_new: float32 [2, 384, 1536], P(None, 'col', 'row')
- mlp_out_new: float32 [2, 384, 1536], P(None, 'col', 'row')
- attn_bias_new: float32 [2, 2, 384], P(None, None, 'row')
- mlp_bias_new: float32 [2, 1536], P(None, 'row')
- norm_vectors_new: float32 [2, 6, 384], P(None, None, 'col')
- attn_in_first_new: float32 [2, 2, 4, 55296], P(None, 'row', 'col')
- attn_out_first_new: float32 [2, 2, 4, 18432], P(None, 'row', 'col')
- mlp_in_first_new: float32 [2, 384, 1536], P(None, 'col', 'row')
- mlp_out_first_new: float32 [2, 384, 1536], P(None, 'col', 'row')
- attn_bias_first_new: float32 [2, 2, 384], P(None, None, 'row')
- mlp_bias_first_new: float32 [2, 1536], P(None, 'row')
- norm_vectors_first_new: float32 [2, 6, 384], P(None, None, 'col')
- attn_in_second_new: float32 [2, 2, 4, 55296], P(None, 'row', 'col')
- attn_out_second_new: float32 [2, 2, 4, 18432], P(None, 'row', 'col')
- mlp_in_second_new: float32 [2, 384, 1536], P(None, 'col', 'row')
- mlp_out_second_new: float32 [2, 384, 1536], P(None, 'col', 'row')
- attn_bias_second_new: float32 [2, 2, 384], P(None, None, 'row')
- mlp_bias_second_new: float32 [2, 1536], P(None, 'row')
- norm_vectors_second_new: float32 [2, 6, 384], P(None, None, 'col')
The draws below stay inside these ranges and needn't reach their ends.
All inputs are finite; a program needn't handle non-finite values.
Results may differ from the reference program's by a relative error of at most 0.023.
Values may be sent and summed in bfloat16 or wider, within the bound.
A program may use at most 128 MiB of HBM per device.

```python
import math
import jax
import jax.numpy as jnp
from jax import lax

D = 384
HEADS = 6
HEAD_DIM = 64
FF = 1536
SEQ = 197
LAYERS = 2
STEP = 10
TOKENS = 12608
N_ROW = 2
N_COL = 4


def draw_images(key, part):
    key = jax.random.fold_in(key, 11)
    column = jnp.arange(D, dtype=jnp.float32) / (D - 1)
    noise = jnp.clip(jax.random.normal(key, (TOKENS, D), jnp.float32), -6.0, 6.0)
    factor = jnp.exp(column * math.log(3.0))
    return (0.5 * noise * factor).astype(jnp.bfloat16)


def draw_norm_vectors(key, part):
    key = jax.random.fold_in(key, 23)
    key_gain, key_shift = jax.random.split(key)
    gains = jax.random.uniform(key_gain, (LAYERS, 6, D), jnp.float32, 0.6, 1.4)
    shifts = jnp.clip(0.3 * jax.random.normal(key_shift, (LAYERS, 6, D), jnp.float32), -0.9, 0.9)
    row_ids = jnp.arange(6)[None, :, None]
    return jnp.where((row_ids == 0) | (row_ids == 3), gains, shifts)


def block_levels(own_key, shape, shards, smallest, high):
    level = 1.0
    for axis_at, shards_of in shards:
        heights = jax.random.uniform(jax.random.fold_in(jax.random.fold_in(own_key, 6), axis_at), (shards_of,), jnp.float32, smallest / len(shards), high / len(shards))
        level = level * jnp.repeat(jnp.exp(heights), shape[axis_at] // shards_of).reshape((-1,) + (1,) * (len(shape) - 1 - axis_at))
    return level


def scatter_about(rng, extent, width, most, pieces=(), held_as=jnp.bfloat16):
    array = jax.random.normal(rng, extent, jnp.float32) * width
    if len(pieces) > 0:
        array = block_levels(rng, extent, pieces, -0.22, 0.18) * array
    return jnp.clip(array, min=-most, max=most).astype(held_as)


def setup_inputs(seed: int = 0) -> dict:
    arg_keys = jax.random.split(jax.random.key(seed), 24)
    return {
        "images": draw_images(jax.random.fold_in(arg_keys[23], 71), 0),
        "cotangent": scatter_about(arg_keys[1], (TOKENS, D), 1.0, 6.0, ((0, 8), (1, 4))),
        "attn_in": scatter_about(arg_keys[2], (LAYERS, N_ROW, N_COL, 3 * D * D // (N_ROW * N_COL)), D ** -0.5, 0.3125, ((1, 2), (2, 4)), jnp.float32),
        "attn_out": scatter_about(arg_keys[3], (LAYERS, N_ROW, N_COL, D * D // (N_ROW * N_COL)), (max(D * 8 // SEQ, 1)) ** -0.5, 1.5, ((1, 2), (2, 4)), jnp.float32),
        "mlp_in": scatter_about(arg_keys[4], (LAYERS, D, FF), D ** -0.5, 0.3125, ((1, 4), (2, 2)), jnp.float32),
        "mlp_out": scatter_about(arg_keys[5], (LAYERS, D, FF), FF ** -0.5, 0.15625, ((1, 4), (2, 2)), jnp.float32),
        "attn_bias": scatter_about(arg_keys[6], (LAYERS, 2, D), 0.3, 1.8, ((2, 2),), jnp.float32),
        "mlp_bias": scatter_about(arg_keys[7], (LAYERS, FF), 0.3, 1.8, ((1, 2),), jnp.float32),
        "norm_vectors": draw_norm_vectors(jax.random.fold_in(arg_keys[23], 71), 0),
        "attn_in_first": scatter_about(arg_keys[9], (LAYERS, N_ROW, N_COL, 3 * D * D // (N_ROW * N_COL)), (0.11 * TOKENS ** 0.5), 74.10833, ((1, 2), (2, 4)), jnp.float32),
        "attn_out_first": scatter_about(arg_keys[10], (LAYERS, N_ROW, N_COL, D * D // (N_ROW * N_COL)), (0.11 * (3 * TOKENS / SEQ) ** 0.5), 9.145228, ((1, 2), (2, 4)), jnp.float32),
        "mlp_in_first": scatter_about(arg_keys[11], (LAYERS, D, FF), (0.033 * TOKENS ** 0.5), 22.45707, ((1, 4), (2, 2)), jnp.float32),
        "mlp_out_first": scatter_about(arg_keys[12], (LAYERS, D, FF), (0.066 * TOKENS ** 0.5), 44.91414, ((1, 4), (2, 2)), jnp.float32),
        "attn_bias_first": scatter_about(arg_keys[13], (LAYERS, 2, D), (0.11 * TOKENS ** 0.5), 74.10833, ((2, 2),), jnp.float32),
        "mlp_bias_first": scatter_about(arg_keys[14], (LAYERS, FF), (0.033 * TOKENS ** 0.5), 22.45707, ((1, 2),), jnp.float32),
        "norm_vectors_first": scatter_about(arg_keys[15], (LAYERS, 6, D), (0.11 * TOKENS ** 0.5), 74.10833, ((2, 4),), jnp.float32),
        "attn_in_second": jnp.clip(jnp.exp(math.log(100.864) - 2.7725887 * jax.random.uniform(arg_keys[16], (LAYERS, N_ROW, N_COL, 3 * D * D // (N_ROW * N_COL)), jnp.float32) ** block_levels(arg_keys[16], (LAYERS, N_ROW, N_COL, 3 * D * D // (N_ROW * N_COL)), ((1, 2), (2, 4)), -0.2, 0.2)), 6.304, 100.864),
        "attn_out_second": jnp.clip(jnp.exp(math.log(1.536) - 2.7725887 * jax.random.uniform(arg_keys[17], (LAYERS, N_ROW, N_COL, D * D // (N_ROW * N_COL)), jnp.float32) ** block_levels(arg_keys[17], (LAYERS, N_ROW, N_COL, D * D // (N_ROW * N_COL)), ((1, 2), (2, 4)), -0.2, 0.2)), 0.096, 1.536),
        "mlp_in_second": jnp.clip(jnp.exp(math.log(9.07776) - 2.7725887 * jax.random.uniform(arg_keys[18], (LAYERS, D, FF), jnp.float32) ** block_levels(arg_keys[18], (LAYERS, D, FF), ((1, 4), (2, 2)), -0.2, 0.2)), 0.56736, 9.07776),
        "mlp_out_second": jnp.clip(jnp.exp(math.log(36.5632) - 2.7795092 * jax.random.uniform(arg_keys[19], (LAYERS, D, FF), jnp.float32) ** block_levels(arg_keys[19], (LAYERS, D, FF), ((1, 4), (2, 2)), -0.2, 0.2)), 2.26944, 36.5632),
        "attn_bias_second": jnp.clip(jnp.exp(math.log(100.864) - 2.7725887 * jax.random.uniform(arg_keys[20], (LAYERS, 2, D), jnp.float32) ** block_levels(arg_keys[20], (LAYERS, 2, D), ((2, 2),), -0.2, 0.2)), 6.304, 100.864),
        "mlp_bias_second": jnp.clip(jnp.exp(math.log(9.07776) - 2.7725887 * jax.random.uniform(arg_keys[21], (LAYERS, FF), jnp.float32) ** block_levels(arg_keys[21], (LAYERS, FF), ((1, 2),), -0.2, 0.2)), 0.56736, 9.07776),
        "norm_vectors_second": jnp.clip(jnp.exp(math.log(100.864) - 2.7725887 * jax.random.uniform(arg_keys[22], (LAYERS, 6, D), jnp.float32) ** block_levels(arg_keys[22], (LAYERS, 6, D), ((2, 4),), -0.2, 0.2)), 6.304, 100.864),
    }


highest = lax.Precision.HIGHEST
norm_eps = 1e-06
beta_one = 0.9
beta_two = 0.999
adam_eps = 1e-08
matrix_rate = 0.15
vector_rate = 0.4
decay_rate = 0.05

@jax.custom_vjp
def low(v):
    return lax.optimization_barrier(v.astype(jnp.bfloat16)).astype(jnp.float32)

@jax.custom_vjp
def low_back(v):
    return v

def low_keep(v):
    return (low(v), None)

def low_pass(kept, grad):
    return (grad,)

def back_keep(v):
    return (v, None)

def back_low(kept, grad):
    return (low(grad),)
low.defvjp(low_keep, low_pass)
low_back.defvjp(back_keep, back_low)

def matmul(left_side, right_side):
    return jnp.dot(left_side, right_side, precision=highest)

def unblock_in(blocks):
    shaped = blocks.reshape(N_ROW, N_COL, D // N_COL, 3, D // N_ROW)
    return shaped.transpose(1, 2, 3, 0, 4).reshape(D, 3, D)

def unblock_out(blocks):
    shaped = blocks.reshape(N_ROW, N_COL, D // N_ROW, D // N_COL)
    return shaped.transpose(0, 2, 1, 3).reshape(D, D)

def layer_norm(values, gain_row, shift_row):
    center = lax.optimization_barrier(jnp.mean(values, axis=-1, keepdims=True))
    spread = lax.optimization_barrier(jnp.mean(values * values, axis=-1, keepdims=True)) - center * center
    scaled = (values - center) * lax.rsqrt(spread + norm_eps)
    return scaled * gain_row + shift_row

def attention(joined_rows):
    split_heads = joined_rows.reshape(-1, SEQ, 3, HEADS, HEAD_DIM)
    queries = split_heads[:, :, 0]
    key_rows = split_heads[:, :, 1]
    values = split_heads[:, :, 2]
    scores = low_back(jnp.einsum('bqhd,bkhd->bhqk', queries, key_rows, precision=highest) * HEAD_DIM ** (-0.5))
    row_max = lax.optimization_barrier(jnp.max(scores, axis=-1, keepdims=True))
    exp_scores = jnp.exp(scores - row_max)
    attn_probs = low(exp_scores / lax.optimization_barrier(jnp.sum(exp_scores, axis=-1, keepdims=True)))
    mixed_rows = jnp.einsum('bhqk,bkhd->bqhd', attn_probs, values, precision=highest)
    return low(low_back(mixed_rows.reshape(-1, D)))

def vit_block(stream, layer_params):
    attn_in, attn_out, mlp_in, mlp_out, attn_bias, mlp_bias, vectors = layer_params
    qkv_full = unblock_in(attn_in)
    proj_full = unblock_out(attn_out)
    normed = low(layer_norm(stream, vectors[0], vectors[1]))
    joined_rows = matmul(normed, low(qkv_full).reshape(D, 3 * D)).reshape(-1, 3, D)
    joined_rows = joined_rows + jnp.stack([attn_bias[0], jnp.zeros_like(attn_bias[0]), attn_bias[1]])
    joined_rows = low(low_back(joined_rows))
    mixed_rows = attention(joined_rows)
    stream = stream + low_back(matmul(mixed_rows, low(proj_full)) + vectors[2])
    normed = low(layer_norm(stream, vectors[3], vectors[4]))
    hidden = low_back(matmul(normed, low(mlp_in)) + mlp_bias)
    act_rows = low(jax.nn.gelu(hidden, approximate=False))
    return stream + low_back(matmul(act_rows, low(mlp_out).T) + vectors[5])

def adam_step(weight, first, second, gradient, rate_now, decay_now):
    first = beta_one * first + (1.0 - beta_one) * gradient
    second = beta_two * second + (1.0 - beta_two) * gradient * gradient
    fixed_first = first / (1.0 - beta_one ** STEP)
    fixed_second = second / (1.0 - beta_two ** STEP)
    weight = weight - rate_now * (fixed_first / (jnp.sqrt(fixed_second) + adam_eps) + decay_now * weight)
    return (weight, first, second)

def reference(images, cotangent, attn_in, attn_out, mlp_in, mlp_out, attn_bias, mlp_bias, norm_vectors, attn_in_first, attn_out_first, mlp_in_first, mlp_out_first, attn_bias_first, mlp_bias_first, norm_vectors_first, attn_in_second, attn_out_second, mlp_in_second, mlp_out_second, attn_bias_second, mlp_bias_second, norm_vectors_second):
    params = (attn_in, attn_out, mlp_in, mlp_out, attn_bias, mlp_bias, norm_vectors)
    firsts = (attn_in_first, attn_out_first, mlp_in_first, mlp_out_first, attn_bias_first, mlp_bias_first, norm_vectors_first)
    seconds = (attn_in_second, attn_out_second, mlp_in_second, mlp_out_second, attn_bias_second, mlp_bias_second, norm_vectors_second)

    def forward(stream, weights):
        for layer_at in range(LAYERS):
            stream = vit_block(stream, tuple((member[layer_at] for member in weights)))
        return stream
    output, pullback = jax.vjp(forward, images.astype(jnp.float32), params)
    input_grad, grads = pullback(cotangent.astype(jnp.float32))
    rates = (matrix_rate, matrix_rate, matrix_rate, matrix_rate, vector_rate, vector_rate, vector_rate)
    decays = (decay_rate, decay_rate, decay_rate, decay_rate, 0.0, 0.0, 0.0)
    updated = [adam_step(params[member], firsts[member], seconds[member], grads[member], rates[member], decays[member]) for member in range(7)]
    return (output.astype(jnp.bfloat16), input_grad, updated[0][0], updated[1][0], updated[2][0], updated[3][0], updated[4][0], updated[5][0], updated[6][0], updated[0][1], updated[1][1], updated[2][1], updated[3][1], updated[4][1], updated[5][1], updated[6][1], updated[0][2], updated[1][2], updated[2][2], updated[3][2], updated[4][2], updated[5][2], updated[6][2])
```

```python
import jax
import jax.numpy as jnp
from jax import lax
from jax.sharding import PartitionSpec as P

D = 384
HEAD_DIM = 64
SEQ = 197
LAYERS = 2
STEP = 10


norm_eps = 1e-06
beta_one = 0.9
beta_two = 0.999
adam_eps = 1e-08
matrix_rate = 0.15
vector_rate = 0.4
decay_rate = 0.05


def gelu_exact(values):
    return jax.nn.gelu(values, approximate=False)


def adam_step(weight, first, second, gradient, rate_now, decay_now):
    first = beta_one * first + (1.0 - beta_one) * gradient
    second = beta_two * second + (1.0 - beta_two) * gradient * gradient
    fixed_first = first / (1.0 - beta_one**STEP)
    fixed_second = second / (1.0 - beta_two**STEP)
    weight = weight - rate_now * (
        fixed_first / (jnp.sqrt(fixed_second) + adam_eps) + decay_now * weight
    )
    return (weight, first, second)


def norm_forward(stream, gain_row, shift_row):
    center = jnp.mean(stream, axis=1, keepdims=True)
    spread = jnp.mean(stream * stream, axis=1, keepdims=True) - center * center
    inverse = lax.rsqrt(spread + norm_eps)
    scaled = (stream - center) * inverse
    return (scaled * gain_row + shift_row, scaled, inverse)


def norm_backward(normed_grad, scaled, inverse, gain_row):
    weighted = normed_grad * gain_row
    stream_grad = inverse * (
        weighted
        - jnp.mean(weighted, axis=1, keepdims=True)
        - scaled * jnp.mean(weighted * scaled, axis=1, keepdims=True)
    )
    return (stream_grad, jnp.sum(normed_grad * scaled, axis=0), jnp.sum(normed_grad, axis=0))


def dot32(form, left, right):
    return jnp.einsum(form, left, right, preferred_element_type=jnp.float32)


def split_joined(joined_low):
    parts = joined_low.shape[0]
    split_heads = joined_low.reshape(parts, -1, SEQ, 3, joined_low.shape[2] // 192, HEAD_DIM)
    return (split_heads[:, :, :, 0], split_heads[:, :, :, 1], split_heads[:, :, :, 2])


def attend(joined_low):
    queries, key_rows, values = split_joined(joined_low)
    scores = dot32("rbqhd,rbkhd->rbhqk", queries, key_rows) * HEAD_DIM ** (-0.5)
    row_max = jnp.max(scores, axis=-1, keepdims=True)
    exp_scores = jnp.exp(scores - row_max)
    probs = exp_scores / jnp.sum(exp_scores, axis=-1, keepdims=True)
    mixed = dot32("rbhqk,rbkhd->rbqhd", probs.astype(jnp.bfloat16), values)
    mixed = mixed.reshape(joined_low.shape[0], joined_low.shape[1], -1)
    return (mixed.astype(jnp.bfloat16), probs)


def attend_back(joined_low, probs, mixed_grad_low):
    queries, key_rows, values = split_joined(joined_low)
    scale = HEAD_DIM ** (-0.5)
    upstream = mixed_grad_low.reshape(queries.shape)
    value_grad = dot32("rbhqk,rbqhd->rbkhd", probs.astype(jnp.bfloat16), upstream)
    prob_grad = dot32("rbqhd,rbkhd->rbhqk", upstream, values)
    score_grad = probs * (prob_grad - jnp.sum(probs * prob_grad, axis=-1, keepdims=True))
    score_low = score_grad.astype(jnp.bfloat16)
    query_grad = dot32("rbhqk,rbkhd->rbqhd", score_low, key_rows) * scale
    key_grad = dot32("rbhqk,rbqhd->rbkhd", score_low, queries) * scale
    stacked = jnp.stack([query_grad, key_grad, value_grad], axis=3)
    return stacked.reshape(joined_low.shape).astype(jnp.bfloat16)


def weight_parts(packed, n_row):
    wr = D // n_row
    hid = (packed.shape[-1] - 4 * wr) // 2
    return (
        packed[..., : 3 * wr],
        packed[..., 3 * wr : 4 * wr],
        packed[..., 4 * wr : 4 * wr + hid],
        packed[..., 4 * wr + hid :],
    )


def layer_forward(stream, packed, vectors, qv_bias, up_bias):
    n_row = packed.shape[0]
    qkv, proj, up, down = weight_parts(packed, n_row)
    normed, scaled_one, inverse_one = norm_forward(stream, vectors[0], vectors[1])
    normed_one = normed.astype(jnp.bfloat16)
    joined = dot32("td,rdk->rtk", normed_one, qkv)
    bias = qv_bias.reshape(2, n_row, 1, -1)
    bias = jnp.concatenate([bias[0], jnp.zeros_like(bias[0]), bias[1]], axis=-1)
    joined_low = (joined + bias).astype(jnp.bfloat16)
    mixed_low, probs = attend(joined_low)
    stream = stream + (dot32("rtk,rdk->td", mixed_low, proj) + vectors[2])
    normed, scaled_two, inverse_two = norm_forward(stream, vectors[3], vectors[4])
    normed_two = normed.astype(jnp.bfloat16)
    hidden = dot32("td,rdk->rtk", normed_two, up) + up_bias.reshape(n_row, 1, -1)
    act_low = gelu_exact(hidden).astype(jnp.bfloat16)
    stream = stream + (dot32("rtk,rdk->td", act_low, down) + vectors[5])
    saved = (
        scaled_one,
        inverse_one,
        normed_one,
        joined_low,
        probs,
        mixed_low,
        scaled_two,
        inverse_two,
        normed_two,
        hidden,
        act_low,
    )
    return stream, saved


def layer_backward(back_grad, packed, vectors, saved):
    (
        scaled_one,
        inverse_one,
        normed_one,
        joined_low,
        probs,
        mixed_low,
        scaled_two,
        inverse_two,
        normed_two,
        hidden,
        act_low,
    ) = saved
    n_row = packed.shape[0]
    qkv, proj, up, down = weight_parts(packed, n_row)
    branch_low = back_grad.astype(jnp.bfloat16)
    down_shift = jnp.sum(branch_low, axis=0, dtype=jnp.float32)
    down_grad = dot32("td,rtk->rdk", branch_low, act_low)
    act_grad = dot32("td,rdk->rtk", branch_low, down)
    hidden_low = jax.vjp(gelu_exact, hidden)[1](act_grad)[0].astype(jnp.bfloat16)
    up_grad = dot32("td,rtk->rdk", normed_two, hidden_low)
    up_shift = jnp.sum(hidden_low, axis=1, dtype=jnp.float32).reshape(-1)
    normed_grad = dot32("rtk,rdk->td", hidden_low, up)
    stream_grad, gain_two, shift_two = norm_backward(
        normed_grad, scaled_two, inverse_two, vectors[3]
    )
    back_grad = back_grad + stream_grad
    branch_low = back_grad.astype(jnp.bfloat16)
    proj_shift = jnp.sum(branch_low, axis=0, dtype=jnp.float32)
    proj_grad = dot32("td,rtk->rdk", branch_low, mixed_low)
    mixed_grad = dot32("td,rdk->rtk", branch_low, proj).astype(jnp.bfloat16)
    joined_grad = attend_back(joined_low, probs, mixed_grad)
    qkv_grad = dot32("td,rtk->rdk", normed_one, joined_grad)
    qkv_shift = jnp.sum(joined_grad, axis=1, dtype=jnp.float32).reshape(n_row, 3, -1)
    normed_grad = dot32("rtk,rdk->td", joined_grad, qkv)
    stream_grad, gain_one, shift_one = norm_backward(
        normed_grad, scaled_one, inverse_one, vectors[0]
    )
    back_grad = back_grad + stream_grad
    packed_grad = jnp.concatenate([qkv_grad, proj_grad, up_grad, down_grad], axis=-1)
    small = jnp.concatenate(
        [
            gain_one,
            shift_one,
            proj_shift,
            gain_two,
            shift_two,
            down_shift,
            qkv_shift[:, 0].reshape(-1),
            qkv_shift[:, 2].reshape(-1),
            up_shift,
        ]
    )
    return back_grad, packed_grad.astype(jnp.bfloat16), small


def per_device(
    images,
    cotangent,
    attn_in,
    attn_out,
    mlp_in,
    mlp_out,
    attn_bias,
    mlp_bias,
    norm_vectors,
    *states,
):
    firsts, seconds = states[:7], states[7:]
    n_row, n_col = lax.axis_size("row"), lax.axis_size("col")
    wc, wr = D // n_col, D // n_row
    hid = mlp_in.shape[2]
    packed = jnp.concatenate(
        [
            attn_in.reshape(LAYERS, wc, 3 * wr),
            attn_out.reshape(LAYERS, wr, wc).transpose(0, 2, 1),
            mlp_in,
            mlp_out,
        ],
        axis=2,
    ).astype(jnp.bfloat16)
    weights = [
        lax.all_gather(packed[at], ("row", "col"), axis=0).reshape(n_row, D, -1)
        for at in range(LAYERS)
    ]
    stream_low = lax.all_to_all(images, "col", split_axis=0, concat_axis=1, tiled=True)
    back_low = lax.all_to_all(cotangent, "col", split_axis=0, concat_axis=1, tiled=True)
    vectors_all = lax.all_gather(norm_vectors, "col", axis=2, tiled=True)
    biases_all = lax.all_gather(
        jnp.concatenate([attn_bias.reshape(LAYERS, -1), mlp_bias], axis=1), "row", axis=0
    )
    qv_all = biases_all[:, :, : 2 * wr].reshape(n_row, LAYERS, 2, wr).transpose(1, 2, 0, 3)
    up_all = biases_all[:, :, 2 * wr :].transpose(1, 0, 2)
    stream = stream_low.astype(jnp.float32)
    saved = []
    for at in range(LAYERS):
        stream, kept = layer_forward(stream, weights[at], vectors_all[at], qv_all[at], up_all[at])
        saved.append(kept)
    activations = lax.all_to_all(
        stream.astype(jnp.bfloat16), "col", split_axis=1, concat_axis=0, tiled=True
    )
    back = back_low.astype(jnp.float32)
    grads, smalls = [None] * LAYERS, [None] * LAYERS
    for at in reversed(range(LAYERS)):
        back, packed_grad, smalls[at] = layer_backward(
            back, weights[at], vectors_all[at], saved[at]
        )
        part = lax.psum_scatter(
            packed_grad.reshape(n_row * n_col, wc, -1), ("row", "col"), scatter_dimension=0
        )
        grads[at] = lax.psum(part, "dp").astype(jnp.float32)
    input_grad = lax.all_to_all(
        back.astype(jnp.bfloat16), "col", split_axis=1, concat_axis=0, tiled=True
    ).astype(jnp.float32)
    small = lax.psum(jnp.stack(smalls), ("dp", "row", "col"))
    me_row, me_col = lax.axis_index("row"), lax.axis_index("col")
    vector_grad = lax.dynamic_slice_in_dim(
        small[:, : 6 * D].reshape(LAYERS, 6, D), me_col * wc, wc, axis=2
    )
    bias_grad = lax.dynamic_slice_in_dim(
        small[:, 6 * D : 8 * D].reshape(LAYERS, 2, D), me_row * wr, wr, axis=2
    )
    up_bias_grad = lax.dynamic_slice_in_dim(small[:, 8 * D :], me_row * hid, hid, axis=1)
    summed = jnp.stack(grads)
    qkv_g, proj_g, up_g, down_g = weight_parts(summed, n_row)
    all_grads = (
        qkv_g.reshape(attn_in.shape),
        proj_g.transpose(0, 2, 1).reshape(attn_out.shape),
        up_g,
        down_g,
        bias_grad,
        up_bias_grad,
        vector_grad,
    )
    params = (attn_in, attn_out, mlp_in, mlp_out, attn_bias, mlp_bias, norm_vectors)
    results = [
        adam_step(
            params[at],
            firsts[at],
            seconds[at],
            all_grads[at],
            matrix_rate if at < 4 else vector_rate,
            decay_rate if at < 4 else 0.0,
        )
        for at in range(7)
    ]
    return (activations, input_grad) + tuple(
        results[at][member] for member in range(3) for at in range(7)
    )


def solution(mesh):
    return jax.shard_map(
        per_device,
        mesh=mesh,
        in_specs=(
            P(("dp", "row"), "col"),
            P(("dp", "row"), "col"),
            P(None, "row", "col", None),
            P(None, "row", "col", None),
            P(None, "col", "row"),
            P(None, "col", "row"),
            P(None, None, "row"),
            P(None, "row"),
            P(None, None, "col"),
            P(None, "row", "col", None),
            P(None, "row", "col", None),
            P(None, "col", "row"),
            P(None, "col", "row"),
            P(None, None, "row"),
            P(None, "row"),
            P(None, None, "col"),
            P(None, "row", "col", None),
            P(None, "row", "col", None),
            P(None, "col", "row"),
            P(None, "col", "row"),
            P(None, None, "row"),
            P(None, "row"),
            P(None, None, "col"),
        ),
        out_specs=(
            P(("dp", "row"), "col"),
            P(("dp", "row"), "col"),
            P(None, "row", "col", None),
            P(None, "row", "col", None),
            P(None, "col", "row"),
            P(None, "col", "row"),
            P(None, None, "row"),
            P(None, "row"),
            P(None, None, "col"),
            P(None, "row", "col", None),
            P(None, "row", "col", None),
            P(None, "col", "row"),
            P(None, "col", "row"),
            P(None, None, "row"),
            P(None, "row"),
            P(None, None, "col"),
            P(None, "row", "col", None),
            P(None, "row", "col", None),
            P(None, "col", "row"),
            P(None, "col", "row"),
            P(None, None, "row"),
            P(None, "row"),
            P(None, None, "col"),
        ),
        check_vma=False,
    )
```

```python
import functools

import jax
import jax.numpy as jnp
from jax import lax
from jax.experimental import pallas as pl
from jax.experimental.pallas import tpu as pltpu
from jax.sharding import PartitionSpec as P

D = 384
HEAD_DIM = 64
SEQ = 197
LAYERS = 2
STEP = 10


norm_eps = 1e-06
beta_one = 0.9
beta_two = 0.999
adam_eps = 1e-08
matrix_rate = 0.15
vector_rate = 0.4
decay_rate = 0.05


def gelu_exact(values):
    return jax.nn.gelu(values, approximate=False)


def adam_step(weight, first, second, gradient, rate_now, decay_now):
    first = beta_one * first + (1.0 - beta_one) * gradient
    second = beta_two * second + (1.0 - beta_two) * gradient * gradient
    fixed_first = first / (1.0 - beta_one**STEP)
    fixed_second = second / (1.0 - beta_two**STEP)
    weight = weight - rate_now * (
        fixed_first / (jnp.sqrt(fixed_second) + adam_eps) + decay_now * weight
    )
    return (weight, first, second)


def norm_forward(stream, gain_row, shift_row):
    center = jnp.mean(stream, axis=1, keepdims=True)
    spread = jnp.mean(stream * stream, axis=1, keepdims=True) - center * center
    inverse = lax.rsqrt(spread + norm_eps)
    scaled = (stream - center) * inverse
    return (scaled * gain_row + shift_row, scaled, inverse)


def norm_backward(normed_grad, scaled, inverse, gain_row):
    weighted = normed_grad * gain_row
    stream_grad = inverse * (
        weighted
        - jnp.mean(weighted, axis=1, keepdims=True)
        - scaled * jnp.mean(weighted * scaled, axis=1, keepdims=True)
    )
    return (stream_grad, jnp.sum(normed_grad * scaled, axis=0), jnp.sum(normed_grad, axis=0))


def dot32(form, left, right):
    return jnp.einsum(form, left, right, preferred_element_type=jnp.float32)


def split_joined(joined_low):
    parts = joined_low.shape[0]
    split_heads = joined_low.reshape(parts, -1, SEQ, 3, joined_low.shape[2] // 192, HEAD_DIM)
    return (split_heads[:, :, :, 0], split_heads[:, :, :, 1], split_heads[:, :, :, 2])


def attend(joined_low):
    queries, key_rows, values = split_joined(joined_low)
    scores = dot32("rbqhd,rbkhd->rbhqk", queries, key_rows) * HEAD_DIM ** (-0.5)
    row_max = jnp.max(scores, axis=-1, keepdims=True)
    exp_scores = jnp.exp(scores - row_max)
    probs = exp_scores / jnp.sum(exp_scores, axis=-1, keepdims=True)
    mixed = dot32("rbhqk,rbkhd->rbqhd", probs.astype(jnp.bfloat16), values)
    mixed = mixed.reshape(joined_low.shape[0], joined_low.shape[1], -1)
    return (mixed.astype(jnp.bfloat16), probs)


def attend_back(joined_low, probs, mixed_grad_low):
    queries, key_rows, values = split_joined(joined_low)
    scale = HEAD_DIM ** (-0.5)
    upstream = mixed_grad_low.reshape(queries.shape)
    value_grad = dot32("rbhqk,rbqhd->rbkhd", probs.astype(jnp.bfloat16), upstream)
    prob_grad = dot32("rbqhd,rbkhd->rbhqk", upstream, values)
    score_grad = probs * (prob_grad - jnp.sum(probs * prob_grad, axis=-1, keepdims=True))
    score_low = score_grad.astype(jnp.bfloat16)
    query_grad = dot32("rbhqk,rbkhd->rbqhd", score_low, key_rows) * scale
    key_grad = dot32("rbhqk,rbqhd->rbkhd", score_low, queries) * scale
    stacked = jnp.stack([query_grad, key_grad, value_grad], axis=3)
    return stacked.reshape(joined_low.shape).astype(jnp.bfloat16)


def weight_parts(packed, n_row):
    wr = D // n_row
    hid = (packed.shape[-1] - 4 * wr) // 2
    return (
        packed[..., : 3 * wr],
        packed[..., 3 * wr : 4 * wr],
        packed[..., 4 * wr : 4 * wr + hid],
        packed[..., 4 * wr + hid :],
    )


def layer_forward(stream, packed, vectors, qv_bias, up_bias):
    n_row = packed.shape[0]
    qkv, proj, up, down = weight_parts(packed, n_row)
    normed, scaled_one, inverse_one = norm_forward(stream, vectors[0], vectors[1])
    normed_one = normed.astype(jnp.bfloat16)
    joined = dot32("td,rdk->rtk", normed_one, qkv)
    bias = qv_bias.reshape(2, n_row, 1, -1)
    bias = jnp.concatenate([bias[0], jnp.zeros_like(bias[0]), bias[1]], axis=-1)
    joined_low = (joined + bias).astype(jnp.bfloat16)
    mixed_low, probs = attend(joined_low)
    stream = stream + (dot32("rtk,rdk->td", mixed_low, proj) + vectors[2])
    normed, scaled_two, inverse_two = norm_forward(stream, vectors[3], vectors[4])
    normed_two = normed.astype(jnp.bfloat16)
    hidden = dot32("td,rdk->rtk", normed_two, up) + up_bias.reshape(n_row, 1, -1)
    act_low = gelu_exact(hidden).astype(jnp.bfloat16)
    stream = stream + (dot32("rtk,rdk->td", act_low, down) + vectors[5])
    saved = (
        scaled_one,
        inverse_one,
        normed_one,
        joined_low,
        probs,
        mixed_low,
        scaled_two,
        inverse_two,
        normed_two,
        hidden,
        act_low,
    )
    return stream, saved


def layer_backward(back_grad, packed, vectors, saved):
    (
        scaled_one,
        inverse_one,
        normed_one,
        joined_low,
        probs,
        mixed_low,
        scaled_two,
        inverse_two,
        normed_two,
        hidden,
        act_low,
    ) = saved
    n_row = packed.shape[0]
    qkv, proj, up, down = weight_parts(packed, n_row)
    branch_low = back_grad.astype(jnp.bfloat16)
    down_shift = jnp.sum(branch_low, axis=0, dtype=jnp.float32)
    down_grad = dot32("td,rtk->rdk", branch_low, act_low)
    act_grad = dot32("td,rdk->rtk", branch_low, down)
    hidden_low = jax.vjp(gelu_exact, hidden)[1](act_grad)[0].astype(jnp.bfloat16)
    up_grad = dot32("td,rtk->rdk", normed_two, hidden_low)
    up_shift = jnp.sum(hidden_low, axis=1, dtype=jnp.float32).reshape(-1)
    normed_grad = dot32("rtk,rdk->td", hidden_low, up)
    stream_grad, gain_two, shift_two = norm_backward(
        normed_grad, scaled_two, inverse_two, vectors[3]
    )
    back_grad = back_grad + stream_grad
    branch_low = back_grad.astype(jnp.bfloat16)
    proj_shift = jnp.sum(branch_low, axis=0, dtype=jnp.float32)
    proj_grad = dot32("td,rtk->rdk", branch_low, mixed_low)
    mixed_grad = dot32("td,rdk->rtk", branch_low, proj).astype(jnp.bfloat16)
    joined_grad = attend_back(joined_low, probs, mixed_grad)
    qkv_grad = dot32("td,rtk->rdk", normed_one, joined_grad)
    qkv_shift = jnp.sum(joined_grad, axis=1, dtype=jnp.float32).reshape(n_row, 3, -1)
    normed_grad = dot32("rtk,rdk->td", joined_grad, qkv)
    stream_grad, gain_one, shift_one = norm_backward(
        normed_grad, scaled_one, inverse_one, vectors[0]
    )
    back_grad = back_grad + stream_grad
    packed_grad = jnp.concatenate([qkv_grad, proj_grad, up_grad, down_grad], axis=-1)
    small = jnp.concatenate(
        [
            gain_one,
            shift_one,
            proj_shift,
            gain_two,
            shift_two,
            down_shift,
            qkv_shift[:, 0].reshape(-1),
            qkv_shift[:, 2].reshape(-1),
            up_shift,
        ]
    )
    return back_grad, packed_grad.astype(jnp.bfloat16), small


CHUNK = 16


def greet(axis, count):
    me = lax.axis_index(axis)
    barrier = pltpu.get_barrier_semaphore()
    for away in range(1, count):
        pl.semaphore_signal(
            barrier,
            inc=1,
            device_id={axis: lax.rem(me + away, count)},
            device_id_type=pl.DeviceIdType.MESH,
        )
    pl.semaphore_wait(barrier, count - 1)
    return me


def sum_kernel(axis, count, part_at, x_ref, out_ref, held, send_sems, recv_sems):
    me = greet(axis, count)
    copies = []
    for away in range(1, count):
        peer = lax.rem(me + away, count)
        copy = pltpu.make_async_remote_copy(
            src_ref=x_ref.at[part_at(peer)],
            dst_ref=held.at[away - 1],
            send_sem=send_sems.at[away - 1],
            recv_sem=recv_sems.at[away - 1],
            device_id={axis: peer},
            device_id_type=pl.DeviceIdType.MESH,
        )
        copy.start()
        copies.append(copy)
    for copy in copies:
        copy.wait()
    own_ref = x_ref.at[part_at(me)]
    for lead in range(out_ref.shape[0]):

        def add_chunk(step, carry):
            rows = pl.ds(pl.multiple_of(step * CHUNK, CHUNK), CHUNK)
            total = own_ref[lead, rows, :].astype(jnp.float32)
            for slot in range(count - 1):
                total = total + held[slot, lead, rows, :].astype(jnp.float32)
            out_ref[lead, rows, :] = total.astype(out_ref.dtype)
            return carry

        lax.fori_loop(0, out_ref.shape[1] // CHUNK, add_chunk, 0)


def exchange_sum(values, axis, part_at, out_shape, collective_id):
    count = lax.axis_size(axis)
    return pl.pallas_call(
        functools.partial(sum_kernel, axis, count, part_at),
        out_shape=jax.ShapeDtypeStruct(out_shape, values.dtype),
        in_specs=[pl.BlockSpec(memory_space=pltpu.VMEM)],
        out_specs=pl.BlockSpec(memory_space=pltpu.VMEM),
        scratch_shapes=[
            pltpu.VMEM((count - 1,) + out_shape, values.dtype),
            pltpu.SemaphoreType.DMA((count - 1,)),
            pltpu.SemaphoreType.DMA((count - 1,)),
        ],
        compiler_params=pltpu.CompilerParams(
            collective_id=collective_id, has_side_effects=True, vmem_limit_bytes=40 << 20
        ),
    )(values)


def gather_kernel(axis, count, x_ref, out_ref, send_sems, recv_sems):
    me = greet(axis, count)
    copies = []
    for away in range(1, count):
        copy = pltpu.make_async_remote_copy(
            src_ref=x_ref,
            dst_ref=out_ref.at[me],
            send_sem=send_sems.at[away - 1],
            recv_sem=recv_sems.at[away - 1],
            device_id={axis: lax.rem(me + away, count)},
            device_id_type=pl.DeviceIdType.MESH,
        )
        copy.start()
        copies.append(copy)
    out_ref[me] = x_ref[...]
    for copy in copies:
        copy.wait()


def exchange_gather(values, axis, collective_id):
    count = lax.axis_size(axis)
    return pl.pallas_call(
        functools.partial(gather_kernel, axis, count),
        out_shape=jax.ShapeDtypeStruct((count,) + values.shape, values.dtype),
        in_specs=[pl.BlockSpec(memory_space=pltpu.VMEM)],
        out_specs=pl.BlockSpec(memory_space=pltpu.VMEM),
        scratch_shapes=[
            pltpu.SemaphoreType.DMA((count - 1,)),
            pltpu.SemaphoreType.DMA((count - 1,)),
        ],
        compiler_params=pltpu.CompilerParams(
            collective_id=collective_id, has_side_effects=True, vmem_limit_bytes=40 << 20
        ),
    )(values)


def sum_gradients(grads, n_row, n_col, wc):
    n_dp = lax.axis_size("dp")
    halves = n_dp // LAYERS
    if n_dp % LAYERS or halves == 0 or wc % (CHUNK * halves):
        parts = [
            lax.psum_scatter(
                grad.reshape(n_row * n_col, wc, -1), ("row", "col"), scatter_dimension=0
            )
            for grad in grads
        ]
        return lax.psum(jnp.stack(parts), "dp").astype(jnp.float32)
    width = grads[0].shape[-1]
    rows = wc // halves
    values = exchange_sum(
        jnp.stack(grads),
        "row",
        lambda peer: (slice(None), peer),
        (LAYERS, n_col * wc, width),
        0,
    )
    values = exchange_sum(
        values.reshape(LAYERS, n_col, halves, rows, width),
        "dp",
        lambda peer: (lax.div(peer, halves), slice(None), lax.rem(peer, halves)),
        (n_col, rows, width),
        1,
    )
    values = exchange_sum(
        values.reshape(n_col, 1, rows, width), "col", lambda peer: (peer,), (1, rows, width), 2
    )
    values = exchange_gather(values.reshape(rows, width), "dp", 3)
    return values.reshape(LAYERS, wc, width).astype(jnp.float32)


def per_device(
    images,
    cotangent,
    attn_in,
    attn_out,
    mlp_in,
    mlp_out,
    attn_bias,
    mlp_bias,
    norm_vectors,
    *states,
):
    firsts, seconds = states[:7], states[7:]
    n_row, n_col = lax.axis_size("row"), lax.axis_size("col")
    wc, wr = D // n_col, D // n_row
    hid = mlp_in.shape[2]
    packed = jnp.concatenate(
        [
            attn_in.reshape(LAYERS, wc, 3 * wr),
            attn_out.reshape(LAYERS, wr, wc).transpose(0, 2, 1),
            mlp_in,
            mlp_out,
        ],
        axis=2,
    ).astype(jnp.bfloat16)
    weights = [
        lax.all_gather(packed[at], ("row", "col"), axis=0).reshape(n_row, D, -1)
        for at in range(LAYERS)
    ]
    stream_low = lax.all_to_all(images, "col", split_axis=0, concat_axis=1, tiled=True)
    back_low = lax.all_to_all(cotangent, "col", split_axis=0, concat_axis=1, tiled=True)
    vectors_all = lax.all_gather(norm_vectors, "col", axis=2, tiled=True)
    biases_all = lax.all_gather(
        jnp.concatenate([attn_bias.reshape(LAYERS, -1), mlp_bias], axis=1), "row", axis=0
    )
    qv_all = biases_all[:, :, : 2 * wr].reshape(n_row, LAYERS, 2, wr).transpose(1, 2, 0, 3)
    up_all = biases_all[:, :, 2 * wr :].transpose(1, 0, 2)
    stream = stream_low.astype(jnp.float32)
    saved = []
    for at in range(LAYERS):
        stream, kept = layer_forward(stream, weights[at], vectors_all[at], qv_all[at], up_all[at])
        saved.append(kept)
    activations = lax.all_to_all(
        stream.astype(jnp.bfloat16), "col", split_axis=1, concat_axis=0, tiled=True
    )
    back = back_low.astype(jnp.float32)
    grads, smalls = [None] * LAYERS, [None] * LAYERS
    for at in reversed(range(LAYERS)):
        back, packed_grad, smalls[at] = layer_backward(
            back, weights[at], vectors_all[at], saved[at]
        )
        grads[at] = packed_grad
    input_grad = lax.all_to_all(
        back.astype(jnp.bfloat16), "col", split_axis=1, concat_axis=0, tiled=True
    ).astype(jnp.float32)
    small = lax.psum(jnp.stack(smalls), ("dp", "row", "col"))
    me_row, me_col = lax.axis_index("row"), lax.axis_index("col")
    vector_grad = lax.dynamic_slice_in_dim(
        small[:, : 6 * D].reshape(LAYERS, 6, D), me_col * wc, wc, axis=2
    )
    bias_grad = lax.dynamic_slice_in_dim(
        small[:, 6 * D : 8 * D].reshape(LAYERS, 2, D), me_row * wr, wr, axis=2
    )
    up_bias_grad = lax.dynamic_slice_in_dim(small[:, 8 * D :], me_row * hid, hid, axis=1)
    summed = sum_gradients(grads, n_row, n_col, wc)
    qkv_g, proj_g, up_g, down_g = weight_parts(summed, n_row)
    all_grads = (
        qkv_g.reshape(attn_in.shape),
        proj_g.transpose(0, 2, 1).reshape(attn_out.shape),
        up_g,
        down_g,
        bias_grad,
        up_bias_grad,
        vector_grad,
    )
    params = (attn_in, attn_out, mlp_in, mlp_out, attn_bias, mlp_bias, norm_vectors)
    results = [
        adam_step(
            params[at],
            firsts[at],
            seconds[at],
            all_grads[at],
            matrix_rate if at < 4 else vector_rate,
            decay_rate if at < 4 else 0.0,
        )
        for at in range(7)
    ]
    return (activations, input_grad) + tuple(
        results[at][member] for member in range(3) for at in range(7)
    )


def solution(mesh):
    return jax.shard_map(
        per_device,
        mesh=mesh,
        in_specs=(
            P(("dp", "row"), "col"),
            P(("dp", "row"), "col"),
            P(None, "row", "col", None),
            P(None, "row", "col", None),
            P(None, "col", "row"),
            P(None, "col", "row"),
            P(None, None, "row"),
            P(None, "row"),
            P(None, None, "col"),
            P(None, "row", "col", None),
            P(None, "row", "col", None),
            P(None, "col", "row"),
            P(None, "col", "row"),
            P(None, None, "row"),
            P(None, "row"),
            P(None, None, "col"),
            P(None, "row", "col", None),
            P(None, "row", "col", None),
            P(None, "col", "row"),
            P(None, "col", "row"),
            P(None, None, "row"),
            P(None, "row"),
            P(None, None, "col"),
        ),
        out_specs=(
            P(("dp", "row"), "col"),
            P(("dp", "row"), "col"),
            P(None, "row", "col", None),
            P(None, "row", "col", None),
            P(None, "col", "row"),
            P(None, "col", "row"),
            P(None, None, "row"),
            P(None, "row"),
            P(None, None, "col"),
            P(None, "row", "col", None),
            P(None, "row", "col", None),
            P(None, "col", "row"),
            P(None, "col", "row"),
            P(None, None, "row"),
            P(None, "row"),
            P(None, None, "col"),
            P(None, "row", "col", None),
            P(None, "row", "col", None),
            P(None, "col", "row"),
            P(None, "col", "row"),
            P(None, None, "row"),
            P(None, "row"),
            P(None, None, "col"),
        ),
        check_vma=False,
    )
```

```python
import functools

import jax
import jax.numpy as jnp
from jax import lax
from jax.experimental import pallas as pl
from jax.experimental.pallas import tpu as pltpu
from jax.sharding import PartitionSpec as P

D = 384
HEAD_DIM = 64
SEQ = 197
LAYERS = 2
STEP = 10


norm_eps = 1e-06
beta_one = 0.9
beta_two = 0.999
adam_eps = 1e-08
matrix_rate = 0.15
vector_rate = 0.4
decay_rate = 0.05


def gelu_exact(values):
    return jax.nn.gelu(values, approximate=False)


def adam_step(weight, first, second, gradient, rate_now, decay_now):
    first = beta_one * first + (1.0 - beta_one) * gradient
    second = beta_two * second + (1.0 - beta_two) * gradient * gradient
    fixed_first = first / (1.0 - beta_one**STEP)
    fixed_second = second / (1.0 - beta_two**STEP)
    weight = weight - rate_now * (
        fixed_first / (jnp.sqrt(fixed_second) + adam_eps) + decay_now * weight
    )
    return (weight, first, second)


def norm_forward(stream, gain_row, shift_row):
    center = jnp.mean(stream, axis=1, keepdims=True)
    spread = jnp.mean(stream * stream, axis=1, keepdims=True) - center * center
    inverse = lax.rsqrt(spread + norm_eps)
    scaled = (stream - center) * inverse
    return (scaled * gain_row + shift_row, scaled, inverse)


def norm_backward(normed_grad, scaled, inverse, gain_row):
    weighted = normed_grad * gain_row
    stream_grad = inverse * (
        weighted
        - jnp.mean(weighted, axis=1, keepdims=True)
        - scaled * jnp.mean(weighted * scaled, axis=1, keepdims=True)
    )
    return (stream_grad, jnp.sum(normed_grad * scaled, axis=0), jnp.sum(normed_grad, axis=0))


def dot32(form, left, right):
    return jnp.einsum(form, left, right, preferred_element_type=jnp.float32)


def split_joined(joined_low):
    parts = joined_low.shape[0]
    split_heads = joined_low.reshape(parts, -1, SEQ, 3, joined_low.shape[2] // 192, HEAD_DIM)
    return (split_heads[:, :, :, 0], split_heads[:, :, :, 1], split_heads[:, :, :, 2])


def attend(joined_low):
    queries, key_rows, values = split_joined(joined_low)
    scores = dot32("rbqhd,rbkhd->rbhqk", queries, key_rows) * HEAD_DIM ** (-0.5)
    row_max = jnp.max(scores, axis=-1, keepdims=True)
    exp_scores = jnp.exp(scores - row_max)
    probs = exp_scores / jnp.sum(exp_scores, axis=-1, keepdims=True)
    mixed = dot32("rbhqk,rbkhd->rbqhd", probs.astype(jnp.bfloat16), values)
    mixed = mixed.reshape(joined_low.shape[0], joined_low.shape[1], -1)
    return (mixed.astype(jnp.bfloat16), probs)


def attend_back(joined_low, probs, mixed_grad_low):
    queries, key_rows, values = split_joined(joined_low)
    scale = HEAD_DIM ** (-0.5)
    upstream = mixed_grad_low.reshape(queries.shape)
    value_grad = dot32("rbhqk,rbqhd->rbkhd", probs.astype(jnp.bfloat16), upstream)
    prob_grad = dot32("rbqhd,rbkhd->rbhqk", upstream, values)
    score_grad = probs * (prob_grad - jnp.sum(probs * prob_grad, axis=-1, keepdims=True))
    score_low = score_grad.astype(jnp.bfloat16)
    query_grad = dot32("rbhqk,rbkhd->rbqhd", score_low, key_rows) * scale
    key_grad = dot32("rbhqk,rbqhd->rbkhd", score_low, queries) * scale
    stacked = jnp.stack([query_grad, key_grad, value_grad], axis=3)
    return stacked.reshape(joined_low.shape).astype(jnp.bfloat16)


def weight_parts(packed, n_row):
    wr = D // n_row
    hid = (packed.shape[-1] - 4 * wr) // 2
    return (
        packed[..., : 3 * wr],
        packed[..., 3 * wr : 4 * wr],
        packed[..., 4 * wr : 4 * wr + hid],
        packed[..., 4 * wr + hid :],
    )


def layer_forward(stream, packed, vectors, qv_bias, up_bias):
    n_row = packed.shape[0]
    qkv, proj, up, down = weight_parts(packed, n_row)
    normed, scaled_one, inverse_one = norm_forward(stream, vectors[0], vectors[1])
    normed_one = normed.astype(jnp.bfloat16)
    joined = dot32("td,rdk->rtk", normed_one, qkv)
    bias = qv_bias.reshape(2, n_row, 1, -1)
    bias = jnp.concatenate([bias[0], jnp.zeros_like(bias[0]), bias[1]], axis=-1)
    joined_low = (joined + bias).astype(jnp.bfloat16)
    mixed_low, probs = attend(joined_low)
    stream = stream + (dot32("rtk,rdk->td", mixed_low, proj) + vectors[2])
    normed, scaled_two, inverse_two = norm_forward(stream, vectors[3], vectors[4])
    normed_two = normed.astype(jnp.bfloat16)
    hidden = dot32("td,rdk->rtk", normed_two, up) + up_bias.reshape(n_row, 1, -1)
    act_low = gelu_exact(hidden).astype(jnp.bfloat16)
    stream = stream + (dot32("rtk,rdk->td", act_low, down) + vectors[5])
    saved = (
        scaled_one,
        inverse_one,
        normed_one,
        joined_low,
        probs,
        mixed_low,
        scaled_two,
        inverse_two,
        normed_two,
        hidden,
        act_low,
    )
    return stream, saved


def layer_backward(back_grad, packed, vectors, saved):
    (
        scaled_one,
        inverse_one,
        normed_one,
        joined_low,
        probs,
        mixed_low,
        scaled_two,
        inverse_two,
        normed_two,
        hidden,
        act_low,
    ) = saved
    n_row = packed.shape[0]
    qkv, proj, up, down = weight_parts(packed, n_row)
    branch_low = back_grad.astype(jnp.bfloat16)
    down_shift = jnp.sum(branch_low, axis=0, dtype=jnp.float32)
    down_grad = dot32("td,rtk->rdk", branch_low, act_low)
    act_grad = dot32("td,rdk->rtk", branch_low, down)
    hidden_low = jax.vjp(gelu_exact, hidden)[1](act_grad)[0].astype(jnp.bfloat16)
    up_grad = dot32("td,rtk->rdk", normed_two, hidden_low)
    up_shift = jnp.sum(hidden_low, axis=1, dtype=jnp.float32).reshape(-1)
    normed_grad = dot32("rtk,rdk->td", hidden_low, up)
    stream_grad, gain_two, shift_two = norm_backward(
        normed_grad, scaled_two, inverse_two, vectors[3]
    )
    back_grad = back_grad + stream_grad
    branch_low = back_grad.astype(jnp.bfloat16)
    proj_shift = jnp.sum(branch_low, axis=0, dtype=jnp.float32)
    proj_grad = dot32("td,rtk->rdk", branch_low, mixed_low)
    mixed_grad = dot32("td,rdk->rtk", branch_low, proj).astype(jnp.bfloat16)
    joined_grad = attend_back(joined_low, probs, mixed_grad)
    qkv_grad = dot32("td,rtk->rdk", normed_one, joined_grad)
    qkv_shift = jnp.sum(joined_grad, axis=1, dtype=jnp.float32).reshape(n_row, 3, -1)
    normed_grad = dot32("rtk,rdk->td", joined_grad, qkv)
    stream_grad, gain_one, shift_one = norm_backward(
        normed_grad, scaled_one, inverse_one, vectors[0]
    )
    back_grad = back_grad + stream_grad
    packed_grad = jnp.concatenate([qkv_grad, proj_grad, up_grad, down_grad], axis=-1)
    small = jnp.concatenate(
        [
            gain_one,
            shift_one,
            proj_shift,
            gain_two,
            shift_two,
            down_shift,
            qkv_shift[:, 0].reshape(-1),
            qkv_shift[:, 2].reshape(-1),
            up_shift,
        ]
    )
    return back_grad, packed_grad.astype(jnp.bfloat16), small


CHUNK = 16


def greet(axis, count):
    me = lax.axis_index(axis)
    barrier = pltpu.get_barrier_semaphore()
    for away in range(1, count):
        pl.semaphore_signal(
            barrier,
            inc=1,
            device_id={axis: lax.rem(me + away, count)},
            device_id_type=pl.DeviceIdType.MESH,
        )
    pl.semaphore_wait(barrier, count - 1)
    return me


def sum_kernel(axis, count, part_at, x_ref, out_ref, held, send_sems, recv_sems):
    me = greet(axis, count)
    copies = []
    for away in range(1, count):
        peer = lax.rem(me + away, count)
        copy = pltpu.make_async_remote_copy(
            src_ref=x_ref.at[part_at(peer)],
            dst_ref=held.at[away - 1],
            send_sem=send_sems.at[away - 1],
            recv_sem=recv_sems.at[away - 1],
            device_id={axis: peer},
            device_id_type=pl.DeviceIdType.MESH,
        )
        copy.start()
        copies.append(copy)
    for copy in copies:
        copy.wait()
    own_ref = x_ref.at[part_at(me)]
    for lead in range(out_ref.shape[0]):

        def add_chunk(step, carry):
            rows = pl.ds(pl.multiple_of(step * CHUNK, CHUNK), CHUNK)
            total = own_ref[lead, rows, :].astype(jnp.float32)
            for slot in range(count - 1):
                total = total + held[slot, lead, rows, :].astype(jnp.float32)
            out_ref[lead, rows, :] = total.astype(out_ref.dtype)
            return carry

        lax.fori_loop(0, out_ref.shape[1] // CHUNK, add_chunk, 0)


def exchange_sum(values, axis, part_at, out_shape, collective_id):
    count = lax.axis_size(axis)
    return pl.pallas_call(
        functools.partial(sum_kernel, axis, count, part_at),
        out_shape=jax.ShapeDtypeStruct(out_shape, values.dtype),
        in_specs=[pl.BlockSpec(memory_space=pltpu.VMEM)],
        out_specs=pl.BlockSpec(memory_space=pltpu.VMEM),
        scratch_shapes=[
            pltpu.VMEM((count - 1,) + out_shape, values.dtype),
            pltpu.SemaphoreType.DMA((count - 1,)),
            pltpu.SemaphoreType.DMA((count - 1,)),
        ],
        compiler_params=pltpu.CompilerParams(
            collective_id=collective_id, has_side_effects=True, vmem_limit_bytes=40 << 20
        ),
    )(values)


def gather_kernel(axis, count, x_ref, out_ref, send_sems, recv_sems):
    me = greet(axis, count)
    copies = []
    for away in range(1, count):
        copy = pltpu.make_async_remote_copy(
            src_ref=x_ref,
            dst_ref=out_ref.at[me],
            send_sem=send_sems.at[away - 1],
            recv_sem=recv_sems.at[away - 1],
            device_id={axis: lax.rem(me + away, count)},
            device_id_type=pl.DeviceIdType.MESH,
        )
        copy.start()
        copies.append(copy)
    out_ref[me] = x_ref[...]
    for copy in copies:
        copy.wait()


def exchange_gather(values, axis, collective_id):
    count = lax.axis_size(axis)
    return pl.pallas_call(
        functools.partial(gather_kernel, axis, count),
        out_shape=jax.ShapeDtypeStruct((count,) + values.shape, values.dtype),
        in_specs=[pl.BlockSpec(memory_space=pltpu.VMEM)],
        out_specs=pl.BlockSpec(memory_space=pltpu.VMEM),
        scratch_shapes=[
            pltpu.SemaphoreType.DMA((count - 1,)),
            pltpu.SemaphoreType.DMA((count - 1,)),
        ],
        compiler_params=pltpu.CompilerParams(
            collective_id=collective_id, has_side_effects=True, vmem_limit_bytes=40 << 20
        ),
    )(values)


def sum_gradients(grads, n_row, n_col, wc):
    n_dp = lax.axis_size("dp")
    halves = n_dp // LAYERS
    if n_dp % LAYERS or halves == 0 or wc % (CHUNK * halves):
        parts = [
            lax.psum_scatter(
                grad.reshape(n_row * n_col, wc, -1), ("row", "col"), scatter_dimension=0
            )
            for grad in grads
        ]
        return lax.psum(jnp.stack(parts), "dp").astype(jnp.float32)
    width = grads[0].shape[-1]
    rows = wc // halves
    values = exchange_sum(
        jnp.stack(grads),
        "row",
        lambda peer: (slice(None), peer),
        (LAYERS, n_col * wc, width),
        0,
    )
    values = exchange_sum(
        values.reshape(LAYERS, n_col, halves, rows, width),
        "dp",
        lambda peer: (lax.div(peer, halves), slice(None), lax.rem(peer, halves)),
        (n_col, rows, width),
        1,
    )
    values = exchange_sum(
        values.reshape(n_col, 1, rows, width), "col", lambda peer: (peer,), (1, rows, width), 2
    )
    values = exchange_gather(values.reshape(rows, width), "dp", 3)
    return values.reshape(LAYERS, wc, width).astype(jnp.float32)


def per_device(
    images,
    cotangent,
    attn_in,
    attn_out,
    mlp_in,
    mlp_out,
    attn_bias,
    mlp_bias,
    norm_vectors,
    *states,
):
    firsts, seconds = states[:7], states[7:]
    n_row, n_col = lax.axis_size("row"), lax.axis_size("col")
    wc, wr = D // n_col, D // n_row
    hid = mlp_in.shape[2]
    packed = jnp.concatenate(
        [
            attn_in.reshape(LAYERS, wc, 3 * wr),
            attn_out.reshape(LAYERS, wr, wc).transpose(0, 2, 1),
            mlp_in,
            mlp_out,
        ],
        axis=2,
    ).astype(jnp.bfloat16)
    weights = [
        lax.all_gather(packed[at], ("row", "col"), axis=0).reshape(n_row, D, -1)
        for at in range(LAYERS)
    ]
    stream_low = lax.all_to_all(images, "col", split_axis=0, concat_axis=1, tiled=True)
    back_low = lax.all_to_all(cotangent, "col", split_axis=0, concat_axis=1, tiled=True)
    vectors_all = lax.all_gather(norm_vectors, "col", axis=2, tiled=True)
    biases_all = lax.all_gather(
        jnp.concatenate([attn_bias.reshape(LAYERS, -1), mlp_bias], axis=1), "row", axis=0
    )
    qv_all = biases_all[:, :, : 2 * wr].reshape(n_row, LAYERS, 2, wr).transpose(1, 2, 0, 3)
    up_all = biases_all[:, :, 2 * wr :].transpose(1, 0, 2)
    stream = stream_low.astype(jnp.float32)
    saved = []
    for at in range(LAYERS):
        stream, kept = layer_forward(stream, weights[at], vectors_all[at], qv_all[at], up_all[at])
        saved.append(kept)
    activations = lax.all_to_all(
        stream.astype(jnp.bfloat16), "col", split_axis=1, concat_axis=0, tiled=True
    )
    back = back_low.astype(jnp.float32)
    grads, smalls = [None] * LAYERS, [None] * LAYERS
    for at in reversed(range(LAYERS)):
        back, packed_grad, smalls[at] = layer_backward(
            back, weights[at], vectors_all[at], saved[at]
        )
        grads[at] = packed_grad
    input_grad = lax.all_to_all(
        back.astype(jnp.bfloat16), "col", split_axis=1, concat_axis=0, tiled=True
    ).astype(jnp.float32)
    small = jnp.sum(lax.all_gather(jnp.stack(smalls), ("dp", "row", "col"), axis=0), axis=0)
    me_row, me_col = lax.axis_index("row"), lax.axis_index("col")
    vector_grad = lax.dynamic_slice_in_dim(
        small[:, : 6 * D].reshape(LAYERS, 6, D), me_col * wc, wc, axis=2
    )
    bias_grad = lax.dynamic_slice_in_dim(
        small[:, 6 * D : 8 * D].reshape(LAYERS, 2, D), me_row * wr, wr, axis=2
    )
    up_bias_grad = lax.dynamic_slice_in_dim(small[:, 8 * D :], me_row * hid, hid, axis=1)
    summed = sum_gradients(grads, n_row, n_col, wc)
    qkv_g, proj_g, up_g, down_g = weight_parts(summed, n_row)
    all_grads = (
        qkv_g.reshape(attn_in.shape),
        proj_g.transpose(0, 2, 1).reshape(attn_out.shape),
        up_g,
        down_g,
        bias_grad,
        up_bias_grad,
        vector_grad,
    )
    params = (attn_in, attn_out, mlp_in, mlp_out, attn_bias, mlp_bias, norm_vectors)
    results = [
        adam_step(
            params[at],
            firsts[at],
            seconds[at],
            all_grads[at],
            matrix_rate if at < 4 else vector_rate,
            decay_rate if at < 4 else 0.0,
        )
        for at in range(7)
    ]
    return (activations, input_grad) + tuple(
        results[at][member] for member in range(3) for at in range(7)
    )


def solution(mesh):
    return jax.shard_map(
        per_device,
        mesh=mesh,
        in_specs=(
            P(("dp", "row"), "col"),
            P(("dp", "row"), "col"),
            P(None, "row", "col", None),
            P(None, "row", "col", None),
            P(None, "col", "row"),
            P(None, "col", "row"),
            P(None, None, "row"),
            P(None, "row"),
            P(None, None, "col"),
            P(None, "row", "col", None),
            P(None, "row", "col", None),
            P(None, "col", "row"),
            P(None, "col", "row"),
            P(None, None, "row"),
            P(None, "row"),
            P(None, None, "col"),
            P(None, "row", "col", None),
            P(None, "row", "col", None),
            P(None, "col", "row"),
            P(None, "col", "row"),
            P(None, None, "row"),
            P(None, "row"),
            P(None, None, "col"),
        ),
        out_specs=(
            P(("dp", "row"), "col"),
            P(("dp", "row"), "col"),
            P(None, "row", "col", None),
            P(None, "row", "col", None),
            P(None, "col", "row"),
            P(None, "col", "row"),
            P(None, None, "row"),
            P(None, "row"),
            P(None, None, "col"),
            P(None, "row", "col", None),
            P(None, "row", "col", None),
            P(None, "col", "row"),
            P(None, "col", "row"),
            P(None, None, "row"),
            P(None, "row"),
            P(None, None, "col"),
            P(None, "row", "col", None),
            P(None, "row", "col", None),
            P(None, "col", "row"),
            P(None, "col", "row"),
            P(None, None, "row"),
            P(None, "row"),
            P(None, None, "col"),
        ),
        check_vma=False,
    )
```
